32 devices in a mesh: grp: 2 (over x), dev: 16 (over z, y, core).
Axes of the slice: x: 2, y: 2, z: 4, core: 2. Of those that a mesh axis runs over, the one named last changes fastest.
Arguments:
- queries: bfloat16 [4096, 2048], P(('grp', 'dev')), may hold values from -6 to 6
- key_rows: bfloat16 [4096, 2048], P(('grp', 'dev')), may hold values from -6 to 6
- value_rows: bfloat16 [4096, 2048], P(('grp', 'dev')), may hold values from -6 to 6
- short_taps: bfloat16 [2048, 128], P('dev'), may hold values from -0.5 to 0.5
- decay_rate: float32 [2048, 16], P('dev'), may hold values from 6.1035156e-05 to 0.034
- residues: float32 [2048, 16], P('dev'), may hold values from -1.5 to 1.5
- skip_gain: float32 [2048], P('dev'), may hold values from -3 to 3
Outputs:
- mixed_out: bfloat16 [4096, 2048], P(('grp', 'dev'))
The draws below stay inside these ranges and needn't reach their ends.
All inputs are finite; a program needn't handle non-finite values.
Results may differ from the reference program's by a relative error of at most 0.0085.
Values may be sent and summed in bfloat16 or wider, within the bound.
A program may use at most 128 MiB of HBM per device.

```python
import jax
import jax.numpy as jnp
from jax import lax

CHANNELS = 2048
TAPS = 128
MODES = 16
TOKENS = 4096


def draw_decay_rate(key, part):
    first_key = jax.random.fold_in(key, 11)
    second_key = jax.random.fold_in(key, 23)
    third_key = jax.random.fold_in(key, 37)
    slow_low = jnp.log(0.25 / TOKENS)
    slow_high = jnp.log(2.0 / TOKENS)
    slow_draw = jnp.exp(slow_low + (slow_high - slow_low) * jax.random.uniform(first_key, (CHANNELS, MODES), jnp.float32))
    fast_low = jnp.log(1.0 / 50.0)
    fast_high = jnp.log(1.0 / 30.0)
    fast_draw = jnp.exp(fast_low + (fast_high - fast_low) * jax.random.uniform(second_key, (CHANNELS, MODES), jnp.float32))
    share = 0.5
    chooser = jax.random.uniform(third_key, (CHANNELS, MODES), jnp.float32)
    return jnp.where(chooser < share, slow_draw, fast_draw).astype(jnp.float32)


def block_scale(key, shape, split, low, top_value):
    def one(dim, shards_of):
        steps = jax.random.uniform(jax.random.fold_in(jax.random.fold_in(key, 6), dim), (shards_of,), jnp.float32, low / len(split), top_value / len(split))
        return jnp.repeat(jnp.exp(steps), shape[dim] // shards_of).reshape((-1,) + (1,) * (len(shape) - dim - 1))

    loudness = one(*split[0])
    for cut in split[1:]:
        loudness = loudness * one(*cut)
    return loudness


def noise(own_key, shape, spread, bound, shards=(), kind=jnp.bfloat16):
    result = jax.random.normal(own_key, shape, jnp.float32) * spread
    if len(shards) > 0:
        result = block_scale(own_key, shape, shards, -0.22, 0.18) * result
    return jnp.clip(result, min=-bound, max=bound).astype(kind)


def setup_inputs(seed: int = 0) -> dict:
    streams_of = jax.random.split(jax.random.key(seed), 8)
    return {
        "queries": noise(streams_of[0], (TOKENS, CHANNELS), 1.0, 6.0, ((0, 32),)),
        "key_rows": noise(streams_of[1], (TOKENS, CHANNELS), 1.0, 6.0, ((0, 32),)),
        "value_rows": noise(streams_of[2], (TOKENS, CHANNELS), 1.0, 6.0, ((0, 32),)),
        "short_taps": noise(streams_of[3], (CHANNELS, TAPS), TAPS ** -0.5, 0.5, ((0, 16),)),
        "decay_rate": draw_decay_rate(jax.random.fold_in(streams_of[7], 71), 0),
        "residues": noise(streams_of[5], (CHANNELS, MODES), 0.25, 1.5, ((0, 16),), jnp.float32),
        "skip_gain": noise(streams_of[6], (CHANNELS,), 0.5, 3.0, ((0, 16),), jnp.float32),
    }


def reference(queries, key_rows, value_rows, short_taps, decay_rate, residues, skip_gain):
    length = queries.shape[0]
    padded_len = 2 * length
    gated = (key_rows.astype(jnp.float32) * value_rows.astype(jnp.float32)).astype(jnp.bfloat16)
    block_width = min(128, CHANNELS)
    block_count = CHANNELS // block_width
    by_channel = gated.T.reshape(block_count, block_width, length)
    positions = jnp.arange(length).astype(jnp.float32)

    def one_block(inputs):
        chan_rows, tap_rows, mode_rates, weights, skip_rows = inputs
        tap_spec = jnp.fft.rfft(tap_rows.astype(jnp.float32), n=padded_len, axis=1)
        row_spec = jnp.fft.rfft(chan_rows.astype(jnp.float32), n=padded_len, axis=1)
        filtered = jnp.fft.irfft(row_spec * tap_spec, n=padded_len, axis=1)[:, :length].astype(jnp.bfloat16)
        kernel = jnp.zeros((block_width, length), jnp.float32)
        for mode_index in range(MODES):
            rate_col = mode_rates[:, mode_index:mode_index + 1]
            kernel = kernel + weights[:, mode_index:mode_index + 1] * jnp.sqrt(2.0 * rate_col) * jnp.exp(-rate_col * positions[None, :])
        filtered_f32 = filtered.astype(jnp.float32)
        conv_spec = jnp.fft.rfft(filtered_f32, n=padded_len, axis=1) * jnp.fft.rfft(kernel, n=padded_len, axis=1)
        long_conv = jnp.fft.irfft(conv_spec, n=padded_len, axis=1)[:, :length]
        return (long_conv + skip_rows[:, None] * filtered_f32).astype(jnp.bfloat16)
    carried = lax.map(one_block, (by_channel, short_taps.reshape(block_count, block_width, TAPS), decay_rate.reshape(block_count, block_width, MODES), residues.reshape(block_count, block_width, MODES), skip_gain.reshape(block_count, block_width)))
    carried = carried.reshape(CHANNELS, length).T
    return (queries.astype(jnp.float32) * carried.astype(jnp.float32)).astype(jnp.bfloat16)
```

```python
import functools
import math

import jax
import jax.numpy as jnp
import ml_dtypes
import numpy as np
from jax import lax
from jax.experimental import pallas as pl
from jax.experimental.pallas import tpu as pltpu
from jax.sharding import PartitionSpec as P

LANES = 128
SUB = 8
TILE = 256
f32 = jnp.float32
bf16 = jnp.bfloat16


def split_np(table):
    high = table.astype(ml_dtypes.bfloat16)
    low = (table - high.astype(np.float64)).astype(ml_dtypes.bfloat16)
    return high, low


def tables(block):
    size = 2 * block
    freq = 2 * np.arange(block)[:, None] + 1
    angle = math.pi / size * (freq * np.arange(size)[None, :] % (2 * size))
    forward = np.concatenate([np.cos(angle), -np.sin(angle)], axis=0)
    return split_np(forward), split_np(forward.T / block)


def dot(a, b):
    return jnp.dot(a, b, preferred_element_type=f32)


def exact_dot(high, low, x):
    return dot(high, x) + dot(low, x)


def wide_dot(high, low, x):
    x_high = x.astype(bf16)
    x_low = (x - x_high.astype(f32)).astype(bf16)
    return dot(high, x_high) + dot(low, x_high) + dot(high, x_low)


def times(x, h):
    half = x.shape[0] // 2
    xr, xi, hr, hi = x[:half], x[half:], h[:half], h[half:]
    return jnp.concatenate([xr * hr - xi * hi, xr * hi + xi * hr], axis=0)


def lanes_of(ref):
    return jnp.concatenate([ref[i] for i in range(ref.shape[0])], axis=-1)


def mode_rows(params_ref, taps, modes):
    rows = lanes_of(params_ref.at[:, taps:]).astype(f32)
    rate = rows[:modes] + rows[modes : 2 * modes]
    weight = rows[2 * modes : 3 * modes] + rows[3 * modes : 4 * modes]
    gain = rows[4 * modes : 4 * modes + 1] + rows[4 * modes + 1 : 4 * modes + 2]
    return rate, weight, gain


def modal_rows(rate, start, block, modes, first):
    step = jnp.exp(-SUB * rate)
    rows = (lax.broadcasted_iota(jnp.int32, (SUB, rate.shape[1]), 0) + first).astype(f32)
    totals = [None] * (block // SUB)
    for m in range(modes):
        term = start[m : m + 1] * jnp.exp(-rate[m : m + 1] * rows)
        factor = jnp.broadcast_to(step[m : m + 1], term.shape)
        for i in range(block // SUB):
            totals[i] = term if m == 0 else totals[i] + term
            term = term * factor
    return jnp.concatenate(totals, axis=0)


def short_kernel(modes, taps, prev_ref, own_ref, params_ref, fh, fl, ih, il, filtered_ref, state_ref):
    block = own_ref.shape[0]
    x = jnp.concatenate([prev_ref[...], own_ref[...]], axis=0)
    spec = exact_dot(fh[...], fl[...], x)
    tap_rows = lanes_of(params_ref.at[:, :taps])
    tap_spec = exact_dot(fh[:, :taps], fl[:, :taps], tap_rows)
    filtered = wide_dot(ih[block:], il[block:], times(spec, tap_spec)).astype(bf16)
    filtered_ref[...] = filtered
    filtered = filtered.astype(f32)
    rate, _, _ = mode_rows(params_ref, taps, modes)
    step = jnp.exp(-SUB * rate)
    back = (SUB - 1 - lax.broadcasted_iota(jnp.int32, (SUB, rate.shape[1]), 0)).astype(f32)
    sums = []
    for m in range(modes):
        factor = jnp.broadcast_to(step[m : m + 1], back.shape)
        total = filtered[:SUB]
        for i in range(1, block // SUB):
            total = total * factor + filtered[SUB * i : SUB * i + SUB]
        total = total * jnp.exp(-rate[m : m + 1] * back)
        sums.append(jnp.sum(total, axis=0, keepdims=True))
    state = jnp.concatenate(sums, axis=0)
    for i in range(state_ref.shape[0]):
        state_ref[i] = state[:, LANES * i : LANES * (i + 1)]


def local_kernel(modes, taps, filtered_ref, params_ref, fh, fl, ih, il, out_ref):
    block = filtered_ref.shape[0]
    rate, weight, gain = mode_rows(params_ref, taps, modes)
    kernel = modal_rows(rate, weight, block, modes, 0)
    kernel_spec = wide_dot(fh[:, :block], fl[:, :block], kernel)
    filtered = filtered_ref[...]
    spec = exact_dot(fh[:, :block], fl[:, :block], filtered)
    conv = wide_dot(ih[:block], il[:block], times(spec, kernel_spec))
    out_ref[...] = conv + gain * filtered.astype(f32)


def final_kernel(modes, taps, local_ref, state_ref, params_ref, queries_ref, out_ref):
    block = local_ref.shape[0]
    rate, weight, _ = mode_rows(params_ref, taps, modes)
    start = weight * lanes_of(state_ref)
    carried = (local_ref[...] + modal_rows(rate, start, block, modes, 1)).astype(bf16)
    out_ref[...] = (queries_ref[...].astype(f32) * carried.astype(f32)).astype(bf16)


def scan_kernel(decay_ref, state_ref, out_ref):
    decay = decay_ref[...]

    def step(i, carry):
        out_ref[i] = carry
        return carry * decay + state_ref[i]

    lax.fori_loop(0, state_ref.shape[0], step, jnp.zeros_like(decay))


def split_bf16(x):
    high = lax.reduce_precision(x, 8, 7)
    return [high.astype(bf16), (x - high).astype(bf16)]


def by_tile(x):
    rows, width = x.shape
    return x.reshape(rows, width // LANES, LANES).swapaxes(0, 1)


def shards(queries, key_rows, value_rows, short_taps, decay_rate, residues, skip_gain):
    block, channels = queries.shape
    few, taps = short_taps.shape
    modes = decay_rate.shape[1]
    groups, devs = lax.axis_size("grp"), lax.axis_size("dev")
    both = ("grp", "dev")
    size = groups * devs
    part = modes // groups
    group = lax.axis_index("grp")

    gated = (key_rows.astype(f32) * value_rows.astype(f32)).astype(bf16)
    prev = lax.ppermute(gated, both, [(i, i + 1) for i in range(size - 1)])

    rate_rows = decay_rate.T
    weight_rows = residues.T * jnp.sqrt(2.0 * rate_rows)
    gain_rows = split_bf16(skip_gain[None, :])
    pad = jnp.zeros((modes - 2, few), bf16)
    packed = jnp.concatenate(
        [short_taps.T] + split_bf16(rate_rows) + split_bf16(weight_rows) + gain_rows + [pad], axis=0
    )
    if few % LANES == 0:
        params = lax.all_gather(packed, "dev", axis=0, tiled=False)
        params = params.reshape(devs, -1, few // LANES, LANES).swapaxes(1, 2)
        params = params.reshape(channels // LANES, -1, LANES)
    else:
        params = by_tile(lax.all_gather(packed, "dev", axis=1, tiled=True))

    (fh, fl), (ih, il) = tables(block)
    fixed = [jnp.asarray(t) for t in (fh, fl, ih, il)]
    width = min(TILE, channels)
    grid = (channels // width,)
    tiles = width // LANES
    rows_spec = pl.BlockSpec((block, width), lambda i: (0, i))
    param_spec = pl.BlockSpec((tiles, params.shape[1], LANES), lambda i: (i, 0, 0))
    state_spec = pl.BlockSpec((tiles, modes, LANES), lambda i: (i, 0, 0))
    fixed_specs = [pl.BlockSpec(t.shape, lambda i: (0, 0)) for t in fixed]
    roomy = pltpu.CompilerParams(vmem_limit_bytes=32 * 1024 * 1024)

    def cost(passes):
        return pl.CostEstimate(flops=passes * 4 * block * block * channels, bytes_accessed=3 * block * channels * 2, transcendentals=0)

    filtered, state = pl.pallas_call(
        functools.partial(short_kernel, modes, taps),
        grid=grid,
        in_specs=[rows_spec, rows_spec, param_spec] + fixed_specs,
        out_specs=[rows_spec, state_spec],
        out_shape=[
            jax.ShapeDtypeStruct((block, channels), bf16),
            jax.ShapeDtypeStruct((channels // LANES, modes, LANES), f32),
        ],
        compiler_params=roomy,
        cost_estimate=cost(9),
        name="short",
    )(prev, gated, params, *fixed)

    outgoing = state.swapaxes(0, 1).reshape(groups, part, devs, few).swapaxes(1, 2).reshape(size, part, few)
    incoming = lax.all_to_all(outgoing, both, split_axis=0, concat_axis=0, tiled=True)
    own_decay = jnp.exp(-block * lax.dynamic_slice_in_dim(rate_rows, group * part, part, 0))
    scanned = pl.pallas_call(
        scan_kernel,
        out_shape=jax.ShapeDtypeStruct(incoming.shape, f32),
        name="scan",
    )(own_decay, incoming)
    returned = lax.all_to_all(scanned, both, split_axis=0, concat_axis=0, tiled=True)
    returned = returned.reshape(groups, devs, part, few).swapaxes(1, 2).reshape(modes, channels)
    returned = by_tile(returned)

    local = pl.pallas_call(
        functools.partial(local_kernel, modes, taps),
        grid=grid,
        in_specs=[rows_spec, param_spec] + fixed_specs,
        out_specs=rows_spec,
        out_shape=jax.ShapeDtypeStruct((block, channels), f32),
        compiler_params=roomy,
        cost_estimate=cost(8),
        name="local",
    )(filtered, params, *fixed)

    return pl.pallas_call(
        functools.partial(final_kernel, modes, taps),
        grid=grid,
        in_specs=[rows_spec, state_spec, param_spec, rows_spec],
        out_specs=rows_spec,
        out_shape=jax.ShapeDtypeStruct((block, channels), bf16),
        compiler_params=roomy,
        name="final",
    )(local, returned, params, queries)


def solution(mesh):
    return jax.shard_map(
        shards,
        mesh=mesh,
        in_specs=(
            P(("grp", "dev"), None),
            P(("grp", "dev"), None),
            P(("grp", "dev"), None),
            P("dev", None),
            P("dev", None),
            P("dev", None),
            P("dev"),
        ),
        out_specs=P(("grp", "dev"), None),
        check_vma=False,
    )
```

```python
import functools
import math

import jax
import jax.numpy as jnp
import ml_dtypes
import numpy as np
from jax import lax
from jax.experimental import pallas as pl
from jax.experimental.pallas import tpu as pltpu
from jax.sharding import PartitionSpec as P

SUB = 8
TILE = 256
HALO_CHUNKS = 4
f32 = jnp.float32
bf16 = jnp.bfloat16


def split_np(table):
    high = table.astype(ml_dtypes.bfloat16)
    low = (table - high.astype(np.float64)).astype(ml_dtypes.bfloat16)
    return high, low


def tables(block):
    size = 2 * block
    freq = 2 * np.arange(block)[:, None] + 1
    angle = math.pi / size * (freq * np.arange(size)[None, :] % (2 * size))
    forward = np.concatenate([np.cos(angle), -np.sin(angle)], axis=0)
    return split_np(forward), split_np(forward.T / block)


def dot(a, b):
    return jnp.dot(a, b, preferred_element_type=f32)


def exact_dot(high, low, x):
    return dot(high, x) + dot(low, x)


def wide_dot(high, low, x):
    x_high = x.astype(bf16)
    x_low = (x - x_high.astype(f32)).astype(bf16)
    return dot(high, x_high) + dot(low, x_high) + dot(high, x_low)


def times(x, h):
    half = x.shape[0] // 2
    xr, xi, hr, hi = x[:half], x[half:], h[:half], h[half:]
    return jnp.concatenate([xr * hr - xi * hi, xr * hi + xi * hr], axis=0)


def lanes_of(pieces):
    return jnp.concatenate(pieces, axis=-1)


def modal_rows(rate, start, block, modes, first):
    step = jnp.exp(-SUB * rate)
    rows = (lax.broadcasted_iota(jnp.int32, (SUB, rate.shape[1]), 0) + first).astype(f32)
    totals = [None] * (block // SUB)
    for m in range(modes):
        term = start[m : m + 1] * jnp.exp(-rate[m : m + 1] * rows)
        factor = jnp.broadcast_to(step[m : m + 1], term.shape)
        for i in range(block // SUB):
            totals[i] = term if m == 0 else totals[i] + term
            term = term * factor
    return jnp.concatenate(totals, axis=0)


def spread(part, index):
    return {"grp": index // part, "dev": index % part}


def whole_kernel(
    taps, modes, key_ref, value_ref, packed_ref, decay_ref, fh, fl, ih, il, carried_ref,
    own, prev, params, filtered, local, outgoing, incoming, scanned, returned,
    halo_send, halo_recv, gather_send, gather_recv, out_send, out_recv, back_send, back_recv,
):
    block, channels = own.shape
    groups, devs = lax.axis_size("grp"), lax.axis_size("dev")
    size = groups * devs
    group, dev = lax.axis_index("grp"), lax.axis_index("dev")
    me = group * devs + dev
    few = params.shape[2]
    part = modes // groups
    width = min(TILE, channels)
    tiles = channels // width
    shards_per_tile = width // few

    def remote(src, dst, send, recv, target):
        return pltpu.make_async_remote_copy(
            src_ref=src, dst_ref=dst, send_sem=send, recv_sem=recv,
            device_id=target, device_id_type=pl.DeviceIdType.MESH,
        )

    def lanes(i, span):
        return pl.ds(pl.multiple_of(i * span, span), span)

    barrier = pltpu.get_barrier_semaphore()

    def greet(i, carry):
        pl.semaphore_signal(
            barrier, inc=1, device_id=spread(devs, lax.rem(me + i, size)), device_id_type=pl.DeviceIdType.MESH
        )
        return carry

    lax.fori_loop(1, size, greet, 0)

    params[dev] = packed_ref[...]
    for i in range(tiles):
        cols = slice(i * width, (i + 1) * width)
        own[:, cols] = (key_ref[:, cols].astype(f32) * value_ref[:, cols].astype(f32)).astype(bf16)
    pl.semaphore_wait(barrier, size - 1)

    slow_size = devs // 4
    slow, mid, fast = dev // 4, dev // 2 % 2, dev % 2

    def slot(s, m, f):
        return s * 4 + m * 2 + f

    def gather_copy(index, sem, target_dev):
        return remote(
            params.at[index], params.at[index], gather_send.at[sem], gather_recv.at[sem],
            {"grp": group, "dev": target_dev},
        )

    def first(j):
        return gather_copy(dev, j, slot(lax.rem(slow + j, slow_size), mid, fast))

    def second(j):
        return gather_copy(
            slot(lax.rem(slow - j + slow_size, slow_size), mid, fast), slow_size + j, slot(slow, 1 - mid, fast)
        )

    def third(j, m):
        source = lax.rem(slow - j + slow_size, slow_size)
        middle = mid if m == 0 else 1 - mid
        return gather_copy(slot(source, middle, fast), (2 + m) * slow_size + j, slot(slow, mid, 1 - fast))

    for j in range(1, slow_size):
        first(j).start()
    second(0).start()
    third(0, 0).start()

    next_id = spread(devs, lax.rem(me + 1, size))
    chunks = halo_send.shape[0]
    span = channels // chunks

    def halo(i):
        cols = slice(i * span, (i + 1) * span)
        return remote(own.at[:, cols], prev.at[:, cols], halo_send.at[i], halo_recv.at[i], next_id)

    @pl.when(me < size - 1)
    def _():
        for i in range(chunks):
            halo(i).start()

    for j in range(1, slow_size):
        first(j).wait_recv()
        second(j).start()
        third(j, 0).start()
    for j in range(slow_size):
        second(j).wait_recv()
        third(j, 1).start()
    for j in range(slow_size):
        third(j, 0).wait_recv()
    for j in range(slow_size):
        third(j, 1).wait_recv()

    @pl.when(me == 0)
    def _():
        prev[...] = jnp.zeros_like(prev)

    @pl.when(me > 0)
    def _():
        for i in range(chunks):
            halo(i).wait_recv()

    def tap_rows(i):
        return lanes_of([params[i * shards_per_tile + n, :taps, :] for n in range(shards_per_tile)])

    def mode_rows(i):
        rows = lanes_of([params[i * shards_per_tile + n, taps:, :].astype(f32) for n in range(shards_per_tile)])
        rate = rows[:modes] + rows[modes : 2 * modes]
        weight = rows[2 * modes : 3 * modes] + rows[3 * modes : 4 * modes]
        gain = rows[4 * modes : 4 * modes + 1] + rows[4 * modes + 1 : 4 * modes + 2]
        return rate, weight, gain

    def out_copy(target):
        return remote(
            outgoing.at[target], incoming.at[me], out_send.at[target], out_recv.at[me], spread(devs, target)
        )

    def short_step(i, carry):
        cols = lanes(i, width)
        x = jnp.concatenate([prev[:, cols], own[:, cols]], axis=0)
        spec = exact_dot(fh[...], fl[...], x)
        tap_spec = exact_dot(fh[:, :taps], fl[:, :taps], tap_rows(i))
        rows = wide_dot(ih[block:], il[block:], times(spec, tap_spec)).astype(bf16)
        filtered[:, cols] = rows
        rows = rows.astype(f32)
        rate, _, _ = mode_rows(i)
        step = jnp.exp(-SUB * rate)
        back = (SUB - 1 - lax.broadcasted_iota(jnp.int32, (SUB, width), 0)).astype(f32)
        sums = []
        for m in range(modes):
            factor = jnp.broadcast_to(step[m : m + 1], back.shape)
            total = rows[:SUB]
            for b in range(1, block // SUB):
                total = total * factor + rows[SUB * b : SUB * b + SUB]
            total = total * jnp.exp(-rate[m : m + 1] * back)
            sums.append(jnp.sum(total, axis=0, keepdims=True))
        state = jnp.concatenate(sums, axis=0)
        for n in range(shards_per_tile):
            for g in range(groups):
                target = g * devs + i * shards_per_tile + n
                outgoing[target] = state[g * part : (g + 1) * part, few * n : few * (n + 1)]

                @pl.when(target != me)
                def _():
                    out_copy(target).start()

        return carry

    lax.fori_loop(0, tiles, short_step, 0)

    def local_step(i, carry):
        cols = lanes(i, width)
        rate, weight, gain = mode_rows(i)
        kernel = modal_rows(rate, weight, block, modes, 0)
        kernel_spec = wide_dot(fh[:, :block], fl[:, :block], kernel)
        rows = filtered[:, cols]
        spec = exact_dot(fh[:, :block], fl[:, :block], rows)
        conv = wide_dot(ih[:block], il[:block], times(spec, kernel_spec))
        local[:, cols] = conv + gain * rows.astype(f32)
        return carry

    lax.fori_loop(0, tiles // 2, local_step, 0)

    incoming[me] = outgoing[me]
    decay = decay_ref[...]

    def back_copy(target):
        return remote(
            scanned.at[target], returned.at[me], back_send.at[target], back_recv.at[me], spread(devs, target)
        )

    def arrival(e, send, recv, src, dst):
        return remote(src.at[e], dst.at[e], send.at[e], recv.at[e], spread(devs, e))

    def scan_step(e, carry):
        @pl.when(e != me)
        def _():
            arrival(e, out_send, out_recv, outgoing, incoming).wait_recv()

        scanned[e] = carry

        @pl.when(e != me)
        def _():
            back_copy(e).start()

        return carry * decay + incoming[e]

    lax.fori_loop(0, size, scan_step, jnp.zeros_like(decay))
    returned[me] = scanned[me]

    lax.fori_loop(tiles // 2, tiles, local_step, 0)

    def collect(e, carry):
        @pl.when(e != me)
        def _():
            arrival(e, back_send, back_recv, scanned, returned).wait_recv()

        return carry

    lax.fori_loop(0, size, collect, 0)

    def final_step(i, carry):
        cols = lanes(i, width)
        rate, weight, _ = mode_rows(i)
        state = lanes_of(
            [
                jnp.concatenate([returned[g * devs + i * shards_per_tile + n] for g in range(groups)], axis=0)
                for n in range(shards_per_tile)
            ]
        )
        total = local[:, cols] + modal_rows(rate, weight * state, block, modes, 1)
        carried_ref[:, cols] = total.astype(bf16)
        return carry

    lax.fori_loop(0, tiles, final_step, 0)

    def sent(e, carry):
        @pl.when(e != me)
        def _():
            arrival(e, out_send, out_recv, outgoing, incoming).wait_send()
            arrival(e, back_send, back_recv, scanned, returned).wait_send()

        return carry

    lax.fori_loop(0, size, sent, 0)
    for j in range(1, slow_size):
        first(j).wait_send()
    for j in range(slow_size):
        second(j).wait_send()
        third(j, 0).wait_send()
        third(j, 1).wait_send()

    @pl.when(me < size - 1)
    def _():
        for i in range(chunks):
            halo(i).wait_send()


def split_bf16(x):
    high = lax.reduce_precision(x, 8, 7)
    return [high.astype(bf16), (x - high).astype(bf16)]


def shards(queries, key_rows, value_rows, short_taps, decay_rate, residues, skip_gain):
    block, channels = queries.shape
    few, taps = short_taps.shape
    modes = decay_rate.shape[1]
    groups, devs = lax.axis_size("grp"), lax.axis_size("dev")
    size = groups * devs
    part = modes // groups
    group = lax.axis_index("grp")

    rate_rows = decay_rate.T
    weight_rows = residues.T * jnp.sqrt(2.0 * rate_rows)
    gain_rows = split_bf16(skip_gain[None, :])
    pad = jnp.zeros((modes - 2, few), bf16)
    packed = jnp.concatenate(
        [short_taps.T] + split_bf16(rate_rows) + split_bf16(weight_rows) + gain_rows + [pad], axis=0
    )
    own_decay = jnp.exp(-block * lax.dynamic_slice_in_dim(rate_rows, group * part, part, 0))

    (fh, fl), (ih, il) = tables(block)
    fixed = [jnp.asarray(t) for t in (fh, fl, ih, il)]
    vmem = pl.BlockSpec(memory_space=pltpu.VMEM)
    message = pltpu.VMEM((size, part, few), f32)
    dma = pltpu.SemaphoreType.DMA
    carried = pl.pallas_call(
        functools.partial(whole_kernel, taps, modes),
        in_specs=[vmem] * 8,
        out_specs=vmem,
        out_shape=jax.ShapeDtypeStruct((block, channels), bf16),
        scratch_shapes=[
            pltpu.VMEM((block, channels), bf16),
            pltpu.VMEM((block, channels), bf16),
            pltpu.VMEM((devs,) + packed.shape, bf16),
            pltpu.VMEM((block, channels), bf16),
            pltpu.VMEM((block, channels), f32),
            message, message, message, message,
            dma((HALO_CHUNKS,)), dma((HALO_CHUNKS,)), dma((devs,)), dma((devs,)),
            dma((size,)), dma((size,)), dma((size,)), dma((size,)),
        ],
        compiler_params=pltpu.CompilerParams(
            collective_id=0, has_side_effects=True, vmem_limit_bytes=40 * 1024 * 1024
        ),
        name="whole",
    )(key_rows, value_rows, packed, own_decay, *fixed)
    return (queries.astype(f32) * carried.astype(f32)).astype(bf16)


def solution(mesh):
    return jax.shard_map(
        shards,
        mesh=mesh,
        in_specs=(
            P(("grp", "dev"), None),
            P(("grp", "dev"), None),
            P(("grp", "dev"), None),
            P("dev", None),
            P("dev", None),
            P("dev", None),
            P("dev"),
        ),
        out_specs=P(("grp", "dev"), None),
        check_vma=False,
    )
```

```python
import math

import jax
import jax.numpy as jnp
import ml_dtypes
import numpy as np
from jax import lax
from jax.experimental import pallas as pl
from jax.experimental.pallas import tpu as pltpu
from jax.sharding import PartitionSpec as P

SUB = 8
TILE = 256
f32 = jnp.float32
bf16 = jnp.bfloat16


def tables(block):
    size = 2 * block
    freq = 2 * np.arange(block)[:, None] + 1
    angle = math.pi / size * (freq * np.arange(size)[None, :] % (2 * size))
    forward = np.concatenate([np.cos(angle), -np.sin(angle)], axis=0)
    high = forward.astype(ml_dtypes.bfloat16)
    low = (forward - high.astype(np.float64)).astype(ml_dtypes.bfloat16)
    halves = np.concatenate([high[:, :block], low[:, :block]], axis=1)
    return np.stack([high, halves, (forward.T / block).astype(ml_dtypes.bfloat16)]).astype(np.float32)


def dot(a, b):
    return jnp.dot(a, b, preferred_element_type=f32)


def twice_dot(halves, x):
    return dot(halves, jnp.concatenate([x, x], axis=0))


def turned(x):
    size = x.shape[1]
    eye = lax.broadcasted_iota(jnp.int32, (size, size), 0) == lax.broadcasted_iota(jnp.int32, (size, size), 1)
    eye = jnp.where(eye, 1.0, 0.0).astype(bf16)
    return lax.dot_general(eye, x, (((1,), (1,)), ((), ())), preferred_element_type=f32)


def times(x, h):
    half = x.shape[0] // 2
    xr, xi, hr, hi = x[:half], x[half:], h[:half], h[half:]
    return jnp.concatenate([xr * hr - xi * hi, xr * hi + xi * hr], axis=0)


def lanes_of(pieces):
    return jnp.concatenate(pieces, axis=-1)


def modal_rows(rate, start, block, modes, first):
    step = jnp.exp(-SUB * rate)
    rows = (lax.broadcasted_iota(jnp.int32, (SUB, rate.shape[1]), 0) + first).astype(f32)
    totals = [None] * (block // SUB)
    for m in range(modes):
        term = start[m : m + 1] * jnp.exp(-rate[m : m + 1] * rows)
        factor = jnp.broadcast_to(step[m : m + 1], term.shape)
        for i in range(block // SUB):
            totals[i] = term if m == 0 else totals[i] + term
            term = term * factor
    return jnp.concatenate(totals, axis=0)


def spread(part, index):
    return {"grp": index // part, "dev": index % part}


def whole_kernel(
    key_hbm, value_hbm, taps_hbm, rate_hbm, residue_hbm, gain_hbm, table_hbm, carried_ref,
    key_ref, value_ref, taps_ref, rate_ref, residue_ref, gain_ref, table_ref,
    table, own, prev, params, filtered, tap_spec, local, outgoing, incoming, scanned, returned,
    load_sem, halo_send, halo_recv, gather_send, gather_recv, out_send, out_recv, back_send, back_recv,
):
    block, channels = own.shape
    few, taps = taps_ref.shape
    modes = rate_ref.shape[0]
    groups, devs = lax.axis_size("grp"), lax.axis_size("dev")
    size = groups * devs
    group, dev = lax.axis_index("grp"), lax.axis_index("dev")
    me = group * devs + dev
    part = modes // groups
    width = min(TILE, channels)
    tiles = channels // width
    shards_per_tile = width // few

    def remote(src, dst, send, recv, target):
        return pltpu.make_async_remote_copy(
            src_ref=src, dst_ref=dst, send_sem=send, recv_sem=recv,
            device_id=target, device_id_type=pl.DeviceIdType.MESH,
        )

    def lanes(i, span):
        return pl.ds(pl.multiple_of(i * span, span), span)

    loads = [
        pltpu.make_async_copy(src, dst, load_sem.at[i])
        for i, (src, dst) in enumerate(
            [
                (taps_hbm, taps_ref), (rate_hbm, rate_ref), (residue_hbm, residue_ref), (gain_hbm, gain_ref),
                (key_hbm, key_ref), (value_hbm, value_ref), (table_hbm, table_ref),
            ]
        )
    ]
    for load in loads:
        load.start()

    barrier = pltpu.get_barrier_semaphore()

    def greet(i, carry):
        pl.semaphore_signal(
            barrier, inc=1, device_id=spread(devs, lax.rem(me + i, size)), device_id_type=pl.DeviceIdType.MESH
        )
        return carry

    lax.fori_loop(1, size, greet, 0)

    for load in loads[:4]:
        load.wait()
    rate = rate_ref[...]
    rate_high = rate.astype(bf16)
    rate_low = (rate - rate_high.astype(f32)).astype(bf16).astype(f32)
    rate_high = rate_high.astype(f32)
    weight = residue_ref[...] * jnp.sqrt(2.0 * rate)
    gain = gain_ref[...]
    gain_high = gain.astype(bf16).astype(f32)
    row = lax.broadcasted_iota(jnp.int32, (modes, few), 0)
    gain = jnp.where(row == 0, gain_high, jnp.where(row == 1, gain - gain_high, 0.0))
    params[dev, :taps] = turned(taps_ref[...]).astype(bf16)
    for i, rows in enumerate([rate_high, rate_low, weight, gain]):
        params[dev, taps + i * modes : taps + (i + 1) * modes] = rows.astype(bf16)
    rate = rate_high + rate_low
    own_rate = rate[:part]
    for g in range(1, groups):
        own_rate = jnp.where(group == g, rate[g * part : (g + 1) * part], own_rate)
    decay = jnp.exp(-block * own_rate)
    for load in loads[4:]:
        load.wait()
    table[...] = table_ref[...].astype(bf16)
    for i in range(tiles):
        cols = slice(i * width, (i + 1) * width)
        own[:, cols] = (key_ref[:, cols].astype(f32) * value_ref[:, cols].astype(f32)).astype(bf16)
    pl.semaphore_wait(barrier, size - 1)

    slow_size = devs // 4
    slow, mid, fast = dev // 4, dev // 2 % 2, dev % 2
    crossed = groups == 2
    rows_each = params.shape[1] // 2 if crossed else params.shape[1]

    def slot(s, m, f):
        return s * 4 + m * 2 + f

    def piece(index, whole):
        if whole or not crossed:
            return params.at[index]
        return params.at[index, pl.ds(pl.multiple_of(group * rows_each, 16), rows_each)]

    def gather_copy(index, sem, target_group, target_dev, whole=False):
        return remote(
            piece(index, whole), piece(index, whole), gather_send.at[sem], gather_recv.at[sem],
            {"grp": target_group, "dev": target_dev},
        )

    def source(j, m):
        return slot(lax.rem(slow - j + slow_size, slow_size), mid if m == 0 else 1 - mid, fast)

    def first(j):
        return gather_copy(dev, j, group, slot(lax.rem(slow + j, slow_size), mid, fast))

    def second(j):
        return gather_copy(source(j, 0), slow_size + j, group, slot(slow, 1 - mid, fast))

    def cross(j, m):
        return gather_copy(source(j, m), (2 + m) * slow_size + j, 1 - group, dev)

    def third(j, m):
        return gather_copy(source(j, m), (4 + m) * slow_size + j, group, slot(slow, mid, 1 - fast), True)

    for j in range(1, slow_size):
        first(j).start()
    second(0).start()
    third(0, 0).start()

    next_id = spread(devs, lax.rem(me + 1, size))

    def halo(i):
        return remote(
            own.at[:, lanes(i, width)], prev.at[:, lanes(i, width)], halo_send.at[i], halo_recv.at[i], next_id
        )

    for j in range(1, slow_size):
        first(j).wait_recv()
        second(j).start()
        if crossed:
            cross(j, 0).start()

    @pl.when(me < size - 1)
    def _():
        for i in range(tiles):
            halo(i).start()

    @pl.when(me == 0)
    def _():
        prev[...] = jnp.zeros_like(prev)

    for j in range(1, slow_size):
        if crossed:
            cross(j, 0).wait_recv()
        third(j, 0).start()
    for j in range(slow_size):
        second(j).wait_recv()
        if crossed:
            cross(j, 1).start()
    for j in range(slow_size):
        if crossed:
            cross(j, 1).wait_recv()
        third(j, 1).start()
    for j in range(slow_size):
        third(j, 0).wait_recv()
    for j in range(slow_size):
        third(j, 1).wait_recv()

    def tap_rows(i):
        return lanes_of([params[i * shards_per_tile + n, :taps, :] for n in range(shards_per_tile)])

    def mode_rows(i):
        rows = lanes_of([params[i * shards_per_tile + n, taps:, :].astype(f32) for n in range(shards_per_tile)])
        rate = rows[:modes] + rows[modes : 2 * modes]
        weight = rows[2 * modes : 3 * modes]
        gain = rows[3 * modes : 3 * modes + 1] + rows[3 * modes + 1 : 3 * modes + 2]
        return rate, weight, gain

    def out_copy(target):
        return remote(
            outgoing.at[target], incoming.at[me], out_send.at[target], out_recv.at[me], spread(devs, target)
        )

    def tap_step(i, carry):
        tap_spec[:, lanes(i, width)] = twice_dot(table[1], tap_rows(i))
        return carry

    lax.fori_loop(0, tiles, tap_step, 0)

    def short_step(i, carry):
        cols = lanes(i, width)

        @pl.when(me > 0)
        def _():
            halo(i).wait_recv()

        x = jnp.concatenate([prev[:, cols], own[:, cols]], axis=0)
        spec = dot(table[0], x)
        rows = dot(table[2, block:], times(spec, tap_spec[:, cols]).astype(bf16)).astype(bf16)
        filtered[:, cols] = rows
        rows = rows.astype(f32)
        rate, _, _ = mode_rows(i)
        step = jnp.exp(-SUB * rate)
        back = (SUB - 1 - lax.broadcasted_iota(jnp.int32, (SUB, width), 0)).astype(f32)
        sums = []
        for m in range(modes):
            factor = jnp.broadcast_to(step[m : m + 1], back.shape)
            total = rows[:SUB]
            for b in range(1, block // SUB):
                total = total * factor + rows[SUB * b : SUB * b + SUB]
            total = total * jnp.exp(-rate[m : m + 1] * back)
            sums.append(jnp.sum(total, axis=0, keepdims=True))
        state = jnp.concatenate(sums, axis=0)
        for n in range(shards_per_tile):
            for g in range(groups):
                target = g * devs + i * shards_per_tile + n
                outgoing[target] = state[g * part : (g + 1) * part, few * n : few * (n + 1)]

                @pl.when(target != me)
                def _():
                    out_copy(target).start()

        return carry

    lax.fori_loop(0, tiles, short_step, 0)

    def local_step(i, carry):
        cols = lanes(i, width)
        rate, weight, gain = mode_rows(i)
        kernel = modal_rows(rate, weight, block, modes, 0)
        kernel_spec = twice_dot(table[1], kernel.astype(bf16))
        rows = filtered[:, cols]
        spec = twice_dot(table[1], rows)
        conv = dot(table[2, :block], times(spec, kernel_spec).astype(bf16))
        local[:, cols] = conv + gain * rows.astype(f32)
        return carry

    lax.fori_loop(0, tiles // 2, local_step, 0)

    incoming[me] = outgoing[me]

    def back_copy(target):
        return remote(
            scanned.at[target], returned.at[me], back_send.at[target], back_recv.at[me], spread(devs, target)
        )

    def arrival(e, send, recv, src, dst):
        return remote(src.at[e], dst.at[e], send.at[e], recv.at[e], spread(devs, e))

    def scan_step(e, carry):
        @pl.when(e != me)
        def _():
            arrival(e, out_send, out_recv, outgoing, incoming).wait_recv()

        scanned[e] = carry

        @pl.when(e != me)
        def _():
            back_copy(e).start()

        return carry * decay + incoming[e]

    lax.fori_loop(0, size, scan_step, jnp.zeros_like(decay))
    returned[me] = scanned[me]

    lax.fori_loop(tiles // 2, tiles, local_step, 0)

    def collect(e, carry):
        @pl.when(e != me)
        def _():
            arrival(e, back_send, back_recv, scanned, returned).wait_recv()

        return carry

    lax.fori_loop(0, size, collect, 0)

    def final_step(i, carry):
        cols = lanes(i, width)
        rate, weight, _ = mode_rows(i)
        state = lanes_of(
            [
                jnp.concatenate([returned[g * devs + i * shards_per_tile + n] for g in range(groups)], axis=0)
                for n in range(shards_per_tile)
            ]
        )
        total = local[:, cols] + modal_rows(rate, weight * state, block, modes, 1)
        carried_ref[:, cols] = total.astype(bf16)
        return carry

    lax.fori_loop(0, tiles, final_step, 0)

    def sent(e, carry):
        @pl.when(e != me)
        def _():
            arrival(e, out_send, out_recv, outgoing, incoming).wait_send()
            arrival(e, back_send, back_recv, scanned, returned).wait_send()

        return carry

    lax.fori_loop(0, size, sent, 0)
    for j in range(1, slow_size):
        first(j).wait_send()
    for j in range(slow_size):
        second(j).wait_send()
        for m in range(2):
            third(j, m).wait_send()
            if crossed and (j, m) != (0, 0):
                cross(j, m).wait_send()

    @pl.when(me < size - 1)
    def _():
        for i in range(tiles):
            halo(i).wait_send()


def shards(queries, key_rows, value_rows, short_taps, decay_rate, residues, skip_gain):
    block, channels = queries.shape
    few, taps = short_taps.shape
    modes = decay_rate.shape[1]
    groups, devs = lax.axis_size("grp"), lax.axis_size("dev")
    size = groups * devs
    part = modes // groups
    table = jnp.asarray(tables(block))
    tiles = channels // min(TILE, channels)
    operands = [key_rows, value_rows, short_taps, decay_rate.T, residues.T, skip_gain.reshape(1, few), table]

    vmem = pl.BlockSpec(memory_space=pltpu.VMEM)
    message = pltpu.VMEM((size, part, few), f32)
    dma = pltpu.SemaphoreType.DMA
    carried = pl.pallas_call(
        whole_kernel,
        in_specs=[pl.BlockSpec(memory_space=pl.ANY)] * len(operands),
        out_specs=vmem,
        out_shape=jax.ShapeDtypeStruct((block, channels), bf16),
        scratch_shapes=[pltpu.VMEM(x.shape, x.dtype) for x in operands]
        + [
            pltpu.VMEM(table.shape, bf16),
            pltpu.VMEM((block, channels), bf16),
            pltpu.VMEM((block, channels), bf16),
            pltpu.VMEM((devs, taps + 4 * modes, few), bf16),
            pltpu.VMEM((block, channels), bf16),
            pltpu.VMEM((2 * block, channels), f32),
            pltpu.VMEM((block, channels), f32),
            message, message, message, message,
            dma((len(operands),)), dma((tiles,)), dma((tiles,)), dma((devs // 4 * 6,)), dma((devs // 4 * 6,)),
            dma((size,)), dma((size,)), dma((size,)), dma((size,)),
        ],
        compiler_params=pltpu.CompilerParams(
            collective_id=0, has_side_effects=True, vmem_limit_bytes=56 * 1024 * 1024
        ),
        name="whole",
    )(*operands)
    return (queries.astype(f32) * carried.astype(f32)).astype(bf16)


def solution(mesh):
    return jax.shard_map(
        shards,
        mesh=mesh,
        in_specs=(
            P(("grp", "dev"), None),
            P(("grp", "dev"), None),
            P(("grp", "dev"), None),
            P("dev", None),
            P("dev", None),
            P("dev", None),
            P("dev"),
        ),
        out_specs=P(("grp", "dev"), None),
        check_vma=False,
    )
```

```python
import math

import jax
import jax.numpy as jnp
import ml_dtypes
import numpy as np
from jax import lax
from jax.experimental import pallas as pl
from jax.experimental.pallas import tpu as pltpu
from jax.sharding import PartitionSpec as P

SUB = 8
TILE = 256
GROUP = 4
f32 = jnp.float32
bf16 = jnp.bfloat16


def tables(block):
    size = 2 * block
    freq = 2 * np.arange(block)[:, None] + 1
    angle = math.pi / size * (freq * np.arange(size)[None, :] % (2 * size))
    forward = np.concatenate([np.cos(angle), -np.sin(angle)], axis=0)
    high = forward.astype(ml_dtypes.bfloat16)
    low = (forward - high.astype(np.float64)).astype(ml_dtypes.bfloat16)
    halves = np.concatenate([high[:, :block], low[:, :block]], axis=1)
    return np.stack([high, halves, (forward.T / block).astype(ml_dtypes.bfloat16)]).astype(np.float32)


def dot(a, b):
    return jnp.dot(a, b, preferred_element_type=f32)


def twice_dot(halves, x):
    return dot(halves, jnp.concatenate([x, x], axis=0))


def turned(x):
    size = x.shape[1]
    eye = lax.broadcasted_iota(jnp.int32, (size, size), 0) == lax.broadcasted_iota(jnp.int32, (size, size), 1)
    eye = jnp.where(eye, 1.0, 0.0).astype(bf16)
    return lax.dot_general(eye, x, (((1,), (1,)), ((), ())), preferred_element_type=f32)


def times(x, h):
    half = x.shape[0] // 2
    xr, xi, hr, hi = x[:half], x[half:], h[:half], h[half:]
    return jnp.concatenate([xr * hr - xi * hi, xr * hi + xi * hr], axis=0)


def lanes_of(pieces):
    return jnp.concatenate(pieces, axis=-1)


def modal_rows(rate, start, block, modes, first):
    step = jnp.exp(-SUB * rate)
    rows = (lax.broadcasted_iota(jnp.int32, (SUB, rate.shape[1]), 0) + first).astype(f32)
    totals = [None] * (block // SUB)
    for m in range(modes):
        term = start[m : m + 1] * jnp.exp(-rate[m : m + 1] * rows)
        factor = jnp.broadcast_to(step[m : m + 1], term.shape)
        for i in range(block // SUB):
            totals[i] = term if m == 0 else totals[i] + term
            term = term * factor
    return jnp.concatenate(totals, axis=0)


def spread(part, index):
    return {"grp": index // part, "dev": index % part}


def whole_kernel(
    key_hbm, value_hbm, taps_hbm, rate_hbm, residue_hbm, gain_hbm, table_hbm, query_hbm, out_ref,
    key_ref, value_ref, taps_ref, rate_ref, residue_ref, gain_ref, table_ref, query_ref,
    table, own, prev, params, filtered, tap_spec, local, outgoing, incoming, scanned, returned,
    load_sem, halo_send, halo_recv, gather_send, gather_recv, out_send, out_recv, back_send, back_recv,
):
    block, channels = own.shape
    few, taps = taps_ref.shape
    modes = rate_ref.shape[0]
    groups, devs = lax.axis_size("grp"), lax.axis_size("dev")
    size = groups * devs
    group, dev = lax.axis_index("grp"), lax.axis_index("dev")
    me = group * devs + dev
    part = modes // groups
    width = min(TILE, channels)
    tiles = channels // width
    shards_per_tile = width // few
    batch = math.gcd(GROUP, tiles)

    def remote(src, dst, send, recv, target):
        return pltpu.make_async_remote_copy(
            src_ref=src, dst_ref=dst, send_sem=send, recv_sem=recv,
            device_id=target, device_id_type=pl.DeviceIdType.MESH,
        )

    def lanes(i, span):
        return pl.ds(pl.multiple_of(i * span, span), span)

    loads = [
        pltpu.make_async_copy(src, dst, load_sem.at[i])
        for i, (src, dst) in enumerate(
            [
                (taps_hbm, taps_ref), (rate_hbm, rate_ref), (residue_hbm, residue_ref), (gain_hbm, gain_ref),
                (key_hbm, key_ref), (value_hbm, value_ref), (table_hbm, table_ref), (query_hbm, query_ref),
            ]
        )
    ]
    for load in loads:
        load.start()

    barrier = pltpu.get_barrier_semaphore()

    def greet(i, carry):
        pl.semaphore_signal(
            barrier, inc=1, device_id=spread(devs, lax.rem(me + i, size)), device_id_type=pl.DeviceIdType.MESH
        )
        return carry

    lax.fori_loop(1, size, greet, 0)

    for load in loads[:4]:
        load.wait()
    rate = rate_ref[...]
    rate_high = rate.astype(bf16)
    rate_low = (rate - rate_high.astype(f32)).astype(bf16).astype(f32)
    rate_high = rate_high.astype(f32)
    weight = residue_ref[...] * jnp.sqrt(2.0 * rate)
    gain = gain_ref[...]
    gain_high = gain.astype(bf16).astype(f32)
    row = lax.broadcasted_iota(jnp.int32, (modes, few), 0)
    gain = jnp.where(row == 0, gain_high, jnp.where(row == 1, gain - gain_high, 0.0))
    params[dev, :taps] = turned(taps_ref[...]).astype(bf16)
    for i, rows in enumerate([rate_high, rate_low, weight, gain]):
        params[dev, taps + i * modes : taps + (i + 1) * modes] = rows.astype(bf16)
    rate = rate_high + rate_low
    own_rate = rate[:part]
    for g in range(1, groups):
        own_rate = jnp.where(group == g, rate[g * part : (g + 1) * part], own_rate)
    decay = jnp.exp(-block * own_rate)
    for load in loads[4:7]:
        load.wait()
    table[...] = table_ref[...].astype(bf16)
    for i in range(tiles):
        cols = slice(i * width, (i + 1) * width)
        own[:, cols] = (key_ref[:, cols].astype(f32) * value_ref[:, cols].astype(f32)).astype(bf16)
    pl.semaphore_wait(barrier, size - 1)

    slow_size = devs // 4
    slow, mid, fast = dev // 4, dev // 2 % 2, dev % 2
    crossed = groups == 2
    rows_each = params.shape[1] // 2 if crossed else params.shape[1]

    def slot(s, m, f):
        return s * 4 + m * 2 + f

    def piece(index, whole):
        if whole or not crossed:
            return params.at[index]
        return params.at[index, pl.ds(pl.multiple_of(group * rows_each, 16), rows_each)]

    def gather_copy(index, sem, target_group, target_dev, whole=False):
        return remote(
            piece(index, whole), piece(index, whole), gather_send.at[sem], gather_recv.at[sem],
            {"grp": target_group, "dev": target_dev},
        )

    def source(j, m):
        return slot(lax.rem(slow - j + slow_size, slow_size), mid if m == 0 else 1 - mid, fast)

    def first(j):
        return gather_copy(dev, j, group, slot(lax.rem(slow + j, slow_size), mid, fast))

    def second(j):
        return gather_copy(source(j, 0), slow_size + j, group, slot(slow, 1 - mid, fast))

    def cross(j, m):
        return gather_copy(source(j, m), (2 + m) * slow_size + j, 1 - group, dev)

    def third(j, m):
        return gather_copy(source(j, m), (4 + m) * slow_size + j, group, slot(slow, mid, 1 - fast), True)

    for j in range(1, slow_size):
        first(j).start()
    second(0).start()
    third(0, 0).start()

    next_id = spread(devs, lax.rem(me + 1, size))

    def halo(i):
        return remote(
            own.at[:, lanes(i, width)], prev.at[:, lanes(i, width)], halo_send.at[i], halo_recv.at[i], next_id
        )

    @pl.when(me < size - 1)
    def _():
        for i in range(tiles // 2):
            halo(i).start()

    for j in range(1, slow_size):
        first(j).wait_recv()
        second(j).start()
        if crossed:
            cross(j, 0).start()

    @pl.when(me < size - 1)
    def _():
        for i in range(tiles // 2, tiles):
            halo(i).start()

    @pl.when(me == 0)
    def _():
        prev[...] = jnp.zeros_like(prev)

    for j in range(1, slow_size):
        if crossed:
            cross(j, 0).wait_recv()
        third(j, 0).start()
    for j in range(slow_size):
        second(j).wait_recv()
        if crossed:
            cross(j, 1).start()
    for j in range(slow_size):
        if crossed:
            cross(j, 1).wait_recv()
        third(j, 1).start()
    for j in range(slow_size):
        third(j, 0).wait_recv()
    for j in range(slow_size):
        third(j, 1).wait_recv()

    def tap_rows(i):
        return lanes_of([params[i * shards_per_tile + n, :taps, :] for n in range(shards_per_tile)])

    def mode_rows(i):
        rows = lanes_of([params[i * shards_per_tile + n, taps:, :].astype(f32) for n in range(shards_per_tile)])
        rate = rows[:modes] + rows[modes : 2 * modes]
        weight = rows[2 * modes : 3 * modes]
        gain = rows[3 * modes : 3 * modes + 1] + rows[3 * modes + 1 : 3 * modes + 2]
        return rate, weight, gain

    def out_copy(target):
        return remote(
            outgoing.at[target], incoming.at[me], out_send.at[target], out_recv.at[me], spread(devs, target)
        )

    def tap_step(i, carry):
        tap_spec[:, lanes(i, width)] = twice_dot(table[1], tap_rows(i))
        return carry

    lax.fori_loop(0, tiles, tap_step, 0, unroll=True)

    def short_step(i, carry):
        cols = lanes(i, width)
        x = jnp.concatenate([prev[:, cols], own[:, cols]], axis=0)
        spec = dot(table[0], x)
        rows = dot(table[2, block:], times(spec, tap_spec[:, cols]).astype(bf16)).astype(bf16)
        filtered[:, cols] = rows
        rows = rows.astype(f32)
        rate, _, _ = mode_rows(i)
        step = jnp.exp(-SUB * rate)
        back = (SUB - 1 - lax.broadcasted_iota(jnp.int32, (SUB, width), 0)).astype(f32)
        sums = []
        for m in range(modes):
            factor = jnp.broadcast_to(step[m : m + 1], back.shape)
            total = rows[:SUB]
            for b in range(1, block // SUB):
                total = total * factor + rows[SUB * b : SUB * b + SUB]
            total = total * jnp.exp(-rate[m : m + 1] * back)
            sums.append(jnp.sum(total, axis=0, keepdims=True))
        state = jnp.concatenate(sums, axis=0)
        for n in range(shards_per_tile):
            for g in range(groups):
                target = g * devs + i * shards_per_tile + n
                outgoing[target] = state[g * part : (g + 1) * part, few * n : few * (n + 1)]
        return carry

    def short_group(k, carry):
        base = k * batch

        @pl.when(me > 0)
        def _():
            for n in range(batch):
                halo(base + n).wait_recv()

        lax.fori_loop(0, batch, lambda n, c: short_step(base + n, c), 0, unroll=True)

        def send(n, c):
            for g in range(groups):
                target = g * devs + base * shards_per_tile + n

                @pl.when(target != me)
                def _():
                    out_copy(target).start()

            return c

        lax.fori_loop(0, batch * shards_per_tile, send, 0)
        return carry

    lax.fori_loop(0, tiles // batch, short_group, 0)

    def local_step(i, carry):
        cols = lanes(i, width)
        rate, weight, gain = mode_rows(i)
        kernel = modal_rows(rate, weight, block, modes, 0)
        kernel_spec = twice_dot(table[1], kernel.astype(bf16))
        rows = filtered[:, cols]
        spec = twice_dot(table[1], rows)
        conv = dot(table[2, :block], times(spec, kernel_spec).astype(bf16))
        local[:, cols] = conv + gain * rows.astype(f32)
        return carry

    def local_group(k, carry):
        return lax.fori_loop(0, batch, lambda n, c: local_step(k * batch + n, c), carry, unroll=True)

    lax.fori_loop(0, tiles // batch // 2, local_group, 0)

    incoming[me] = outgoing[me]

    def back_copy(target):
        return remote(
            scanned.at[target], returned.at[me], back_send.at[target], back_recv.at[me], spread(devs, target)
        )

    def arrival(e, send, recv, src, dst):
        return remote(src.at[e], dst.at[e], send.at[e], recv.at[e], spread(devs, e))

    def others(visit):
        def step(i, carry):
            visit(lax.rem(me + i, size))
            return carry

        lax.fori_loop(1, size, step, 0)

    others(lambda e: arrival(e, out_send, out_recv, outgoing, incoming).wait_recv())

    def scan_step(k, carry):
        for n in range(2 * GROUP):
            e = k * 2 * GROUP + n
            scanned[e] = carry
            carry = carry * decay + incoming[e]
        return carry

    lax.fori_loop(0, size // (2 * GROUP), scan_step, jnp.zeros_like(decay))
    others(lambda e: back_copy(e).start())
    returned[me] = scanned[me]

    lax.fori_loop(tiles // batch // 2, tiles // batch, local_group, 0)

    others(lambda e: arrival(e, back_send, back_recv, scanned, returned).wait_recv())

    loads[7].wait()

    def final_step(i, carry):
        cols = lanes(i, width)
        rate, weight, _ = mode_rows(i)
        state = lanes_of(
            [
                jnp.concatenate([returned[g * devs + i * shards_per_tile + n] for g in range(groups)], axis=0)
                for n in range(shards_per_tile)
            ]
        )
        total = local[:, cols] + modal_rows(rate, weight * state, block, modes, 1)
        carried = total.astype(bf16).astype(f32)
        out_ref[:, cols] = (query_ref[:, cols].astype(f32) * carried).astype(bf16)
        return carry

    def final_group(k, carry):
        return lax.fori_loop(0, batch, lambda n, c: final_step(k * batch + n, c), carry, unroll=True)

    lax.fori_loop(0, tiles // batch, final_group, 0)

    others(lambda e: arrival(e, out_send, out_recv, outgoing, incoming).wait_send())
    others(lambda e: arrival(e, back_send, back_recv, scanned, returned).wait_send())
    for j in range(1, slow_size):
        first(j).wait_send()
    for j in range(slow_size):
        second(j).wait_send()
        for m in range(2):
            third(j, m).wait_send()
            if crossed and (j, m) != (0, 0):
                cross(j, m).wait_send()

    @pl.when(me < size - 1)
    def _():
        for i in range(tiles):
            halo(i).wait_send()


def shards(queries, key_rows, value_rows, short_taps, decay_rate, residues, skip_gain):
    block, channels = queries.shape
    few, taps = short_taps.shape
    modes = decay_rate.shape[1]
    groups, devs = lax.axis_size("grp"), lax.axis_size("dev")
    size = groups * devs
    part = modes // groups
    table = jnp.asarray(tables(block))
    tiles = channels // min(TILE, channels)
    operands = [key_rows, value_rows, short_taps, decay_rate.T, residues.T, skip_gain.reshape(1, few), table, queries]

    vmem = pl.BlockSpec(memory_space=pltpu.VMEM)
    message = pltpu.VMEM((size, part, few), f32)
    dma = pltpu.SemaphoreType.DMA
    return pl.pallas_call(
        whole_kernel,
        in_specs=[pl.BlockSpec(memory_space=pl.ANY)] * len(operands),
        out_specs=vmem,
        out_shape=jax.ShapeDtypeStruct((block, channels), bf16),
        scratch_shapes=[pltpu.VMEM(x.shape, x.dtype) for x in operands]
        + [
            pltpu.VMEM(table.shape, bf16),
            pltpu.VMEM((block, channels), bf16),
            pltpu.VMEM((block, channels), bf16),
            pltpu.VMEM((devs, taps + 4 * modes, few), bf16),
            pltpu.VMEM((block, channels), bf16),
            pltpu.VMEM((2 * block, channels), f32),
            pltpu.VMEM((block, channels), f32),
            message, message, message, message,
            dma((len(operands),)), dma((tiles,)), dma((tiles,)), dma((devs // 4 * 6,)), dma((devs // 4 * 6,)),
            dma((size,)), dma((size,)), dma((size,)), dma((size,)),
        ],
        compiler_params=pltpu.CompilerParams(
            collective_id=0, has_side_effects=True, vmem_limit_bytes=56 * 1024 * 1024
        ),
        name="whole",
    )(*operands)


def solution(mesh):
    return jax.shard_map(
        shards,
        mesh=mesh,
        in_specs=(
            P(("grp", "dev"), None),
            P(("grp", "dev"), None),
            P(("grp", "dev"), None),
            P("dev", None),
            P("dev", None),
            P("dev", None),
            P("dev"),
        ),
        out_specs=P(("grp", "dev"), None),
        check_vma=False,
    )
```

```python
import math

import jax
import jax.numpy as jnp
import ml_dtypes
import numpy as np
from jax import lax
from jax.experimental import pallas as pl
from jax.experimental.pallas import tpu as pltpu
from jax.sharding import PartitionSpec as P

SUB = 8
TILE = 256
f32 = jnp.float32
bf16 = jnp.bfloat16


def tables(block):
    size = 2 * block
    freq = 2 * np.arange(block)[:, None] + 1
    angle = math.pi / size * (freq * np.arange(size)[None, :] % (2 * size))
    forward = np.concatenate([np.cos(angle), -np.sin(angle)], axis=0)
    high = forward.astype(ml_dtypes.bfloat16)
    low = (forward - high.astype(np.float64)).astype(ml_dtypes.bfloat16)
    halves = np.concatenate([high[:, :block], low[:, :block]], axis=1)
    return np.stack([high, halves, (forward.T / block).astype(ml_dtypes.bfloat16)]).astype(np.float32)


def dot(a, b):
    return jnp.dot(a, b, preferred_element_type=f32)


def twice_dot(halves, x):
    return dot(halves, jnp.concatenate([x, x], axis=0))


def turned(x):
    size = x.shape[1]
    eye = lax.broadcasted_iota(jnp.int32, (size, size), 0) == lax.broadcasted_iota(jnp.int32, (size, size), 1)
    eye = jnp.where(eye, 1.0, 0.0).astype(bf16)
    return lax.dot_general(eye, x, (((1,), (1,)), ((), ())), preferred_element_type=f32)


def times(x, h):
    half = x.shape[0] // 2
    xr, xi, hr, hi = x[:half], x[half:], h[:half], h[half:]
    return jnp.concatenate([xr * hr - xi * hi, xr * hi + xi * hr], axis=0)


def lanes_of(pieces):
    return jnp.concatenate(pieces, axis=-1)


def modal_rows(rate, start, block, modes, first):
    step = jnp.exp(-SUB * rate)
    rows = (lax.broadcasted_iota(jnp.int32, (SUB, rate.shape[1]), 0) + first).astype(f32)
    totals = [None] * (block // SUB)
    for m in range(modes):
        term = start[m : m + 1] * jnp.exp(-rate[m : m + 1] * rows)
        factor = jnp.broadcast_to(step[m : m + 1], term.shape)
        for i in range(block // SUB):
            totals[i] = term if m == 0 else totals[i] + term
            term = term * factor
    return jnp.concatenate(totals, axis=0)


def spread(part, index):
    return {"grp": index // part, "dev": index % part}


def whole_kernel(
    key_hbm, value_hbm, taps_hbm, rate_hbm, residue_hbm, gain_hbm, table_hbm, carried_ref,
    key_ref, value_ref, taps_ref, rate_ref, residue_ref, gain_ref, table_ref,
    table, own, prev, params, filtered, tap_spec, kernel_spec, local, outgoing, incoming, scanned, returned,
    load_sem, halo_send, halo_recv, gather_send, gather_recv, out_send, out_recv, back_send, back_recv,
):
    block, channels = own.shape
    few, taps = taps_ref.shape
    modes = rate_ref.shape[0]
    groups, devs = lax.axis_size("grp"), lax.axis_size("dev")
    size = groups * devs
    group, dev = lax.axis_index("grp"), lax.axis_index("dev")
    me = group * devs + dev
    part = modes // groups
    width = min(TILE, channels)
    tiles = channels // width
    shards_per_tile = width // few

    def remote(src, dst, send, recv, target):
        return pltpu.make_async_remote_copy(
            src_ref=src, dst_ref=dst, send_sem=send, recv_sem=recv,
            device_id=target, device_id_type=pl.DeviceIdType.MESH,
        )

    def lanes(i, span):
        return pl.ds(pl.multiple_of(i * span, span), span)

    loads = [
        pltpu.make_async_copy(src, dst, load_sem.at[i])
        for i, (src, dst) in enumerate(
            [
                (taps_hbm, taps_ref), (rate_hbm, rate_ref), (residue_hbm, residue_ref), (gain_hbm, gain_ref),
                (key_hbm, key_ref), (value_hbm, value_ref), (table_hbm, table_ref),
            ]
        )
    ]
    for load in loads:
        load.start()

    barrier = pltpu.get_barrier_semaphore()

    def greet(i, carry):
        pl.semaphore_signal(
            barrier, inc=1, device_id=spread(devs, lax.rem(me + i, size)), device_id_type=pl.DeviceIdType.MESH
        )
        return carry

    lax.fori_loop(1, size, greet, 0)

    for load in loads[:4]:
        load.wait()
    rate = rate_ref[...]
    rate_high = rate.astype(bf16)
    rate_low = (rate - rate_high.astype(f32)).astype(bf16).astype(f32)
    rate_high = rate_high.astype(f32)
    weight = residue_ref[...] * jnp.sqrt(2.0 * rate)
    gain = gain_ref[...]
    gain_high = gain.astype(bf16).astype(f32)
    row = lax.broadcasted_iota(jnp.int32, (modes, few), 0)
    gain = jnp.where(row == 0, gain_high, jnp.where(row == 1, gain - gain_high, 0.0))
    params[dev, :taps] = turned(taps_ref[...]).astype(bf16)
    for i, rows in enumerate([rate_high, rate_low, weight, gain]):
        params[dev, taps + i * modes : taps + (i + 1) * modes] = rows.astype(bf16)
    rate = rate_high + rate_low
    own_rate = rate[:part]
    for g in range(1, groups):
        own_rate = jnp.where(group == g, rate[g * part : (g + 1) * part], own_rate)
    decay = jnp.exp(-block * own_rate)
    for load in loads[4:]:
        load.wait()
    table[...] = table_ref[...].astype(bf16)
    for i in range(tiles):
        cols = slice(i * width, (i + 1) * width)
        own[:, cols] = (key_ref[:, cols].astype(f32) * value_ref[:, cols].astype(f32)).astype(bf16)
    pl.semaphore_wait(barrier, size - 1)

    slow_size = devs // 4
    slow, mid, fast = dev // 4, dev // 2 % 2, dev % 2
    crossed = groups == 2
    rows_each = params.shape[1] // 2 if crossed else params.shape[1]

    def slot(s, m, f):
        return s * 4 + m * 2 + f

    def piece(index, whole):
        if whole or not crossed:
            return params.at[index]
        return params.at[index, pl.ds(pl.multiple_of(group * rows_each, 16), rows_each)]

    def gather_copy(index, sem, target_group, target_dev, whole=False):
        return remote(
            piece(index, whole), piece(index, whole), gather_send.at[sem], gather_recv.at[sem],
            {"grp": target_group, "dev": target_dev},
        )

    def source(j, m):
        return slot(lax.rem(slow - j + slow_size, slow_size), mid if m == 0 else 1 - mid, fast)

    def first(j):
        return gather_copy(dev, j, group, slot(lax.rem(slow + j, slow_size), mid, fast))

    def second(j):
        return gather_copy(source(j, 0), slow_size + j, group, slot(slow, 1 - mid, fast))

    def cross(j, m):
        return gather_copy(source(j, m), (2 + m) * slow_size + j, 1 - group, dev)

    def third(j, m):
        return gather_copy(source(j, m), (4 + m) * slow_size + j, group, slot(slow, mid, 1 - fast), True)

    for j in range(1, slow_size):
        first(j).start()
    second(0).start()
    third(0, 0).start()

    next_id = spread(devs, lax.rem(me + 1, size))

    def halo(i):
        return remote(
            own.at[:, lanes(i, width)], prev.at[:, lanes(i, width)], halo_send.at[i], halo_recv.at[i], next_id
        )

    for j in range(1, slow_size):
        first(j).wait_recv()
        second(j).start()
        if crossed:
            cross(j, 0).start()

    @pl.when(me < size - 1)
    def _():
        for i in range(tiles):
            halo(i).start()

    @pl.when(me == 0)
    def _():
        prev[...] = jnp.zeros_like(prev)

    for j in range(1, slow_size):
        if crossed:
            cross(j, 0).wait_recv()
        third(j, 0).start()
    for j in range(slow_size):
        second(j).wait_recv()
        if crossed:
            cross(j, 1).start()
    for j in range(slow_size):
        if crossed:
            cross(j, 1).wait_recv()
        third(j, 1).start()
    for j in range(slow_size):
        third(j, 0).wait_recv()
    for j in range(slow_size):
        third(j, 1).wait_recv()

    def tap_rows(i):
        return lanes_of([params[i * shards_per_tile + n, :taps, :] for n in range(shards_per_tile)])

    def mode_rows(i):
        rows = lanes_of([params[i * shards_per_tile + n, taps:, :].astype(f32) for n in range(shards_per_tile)])
        rate = rows[:modes] + rows[modes : 2 * modes]
        weight = rows[2 * modes : 3 * modes]
        gain = rows[3 * modes : 3 * modes + 1] + rows[3 * modes + 1 : 3 * modes + 2]
        return rate, weight, gain

    def out_copy(target):
        return remote(
            outgoing.at[target], incoming.at[me], out_send.at[target], out_recv.at[me], spread(devs, target)
        )

    def tap_step(i, carry):
        rate, weight, _ = mode_rows(i)
        kernel = modal_rows(rate, weight, block, modes, 0)
        tap_spec[:, lanes(i, width)] = twice_dot(table[1], tap_rows(i))
        kernel_spec[:, lanes(i, width)] = twice_dot(table[1], kernel.astype(bf16))
        return carry

    lax.fori_loop(0, tiles, tap_step, 0)

    def short_step(i, carry):
        cols = lanes(i, width)

        @pl.when(me > 0)
        def _():
            halo(i).wait_recv()

        x = jnp.concatenate([prev[:, cols], own[:, cols]], axis=0)
        spec = dot(table[0], x)
        rows = dot(table[2, block:], times(spec, tap_spec[:, cols]).astype(bf16)).astype(bf16)
        filtered[:, cols] = rows
        rows = rows.astype(f32)
        rate, _, _ = mode_rows(i)
        step = jnp.exp(-SUB * rate)
        back = (SUB - 1 - lax.broadcasted_iota(jnp.int32, (SUB, width), 0)).astype(f32)
        sums = []
        for m in range(modes):
            factor = jnp.broadcast_to(step[m : m + 1], back.shape)
            total = rows[:SUB]
            for b in range(1, block // SUB):
                total = total * factor + rows[SUB * b : SUB * b + SUB]
            total = total * jnp.exp(-rate[m : m + 1] * back)
            sums.append(jnp.sum(total, axis=0, keepdims=True))
        state = jnp.concatenate(sums, axis=0)
        for n in range(shards_per_tile):
            for g in range(groups):
                target = g * devs + i * shards_per_tile + n
                outgoing[target] = state[g * part : (g + 1) * part, few * n : few * (n + 1)]

                @pl.when(target != me)
                def _():
                    out_copy(target).start()

        return carry

    lax.fori_loop(0, tiles, short_step, 0)

    def local_step(i, carry):
        cols = lanes(i, width)
        _, _, gain = mode_rows(i)
        rows = filtered[:, cols]
        spec = twice_dot(table[1], rows)
        conv = dot(table[2, :block], times(spec, kernel_spec[:, cols]).astype(bf16))
        local[:, cols] = conv + gain * rows.astype(f32)
        return carry

    lax.fori_loop(0, tiles // 2, local_step, 0)

    incoming[me] = outgoing[me]

    def back_copy(target):
        return remote(
            scanned.at[target], returned.at[me], back_send.at[target], back_recv.at[me], spread(devs, target)
        )

    def arrival(e, send, recv, src, dst):
        return remote(src.at[e], dst.at[e], send.at[e], recv.at[e], spread(devs, e))

    def others(visit):
        def step(i, carry):
            visit(lax.rem(me + i, size))
            return carry

        lax.fori_loop(1, size, step, 0)

    others(lambda e: arrival(e, out_send, out_recv, outgoing, incoming).wait_recv())

    def scan_step(k, carry):
        for n in range(SUB):
            e = k * SUB + n
            scanned[e] = carry
            carry = carry * decay + incoming[e]
        return carry

    lax.fori_loop(0, size // SUB, scan_step, jnp.zeros_like(decay))
    others(lambda e: back_copy(e).start())
    returned[me] = scanned[me]

    lax.fori_loop(tiles // 2, tiles, local_step, 0)

    others(lambda e: arrival(e, back_send, back_recv, scanned, returned).wait_recv())

    def final_step(i, carry):
        cols = lanes(i, width)
        rate, weight, _ = mode_rows(i)
        state = lanes_of(
            [
                jnp.concatenate([returned[g * devs + i * shards_per_tile + n] for g in range(groups)], axis=0)
                for n in range(shards_per_tile)
            ]
        )
        total = local[:, cols] + modal_rows(rate, weight * state, block, modes, 1)
        carried_ref[:, cols] = total.astype(bf16)
        return carry

    lax.fori_loop(0, tiles, final_step, 0)

    others(lambda e: arrival(e, out_send, out_recv, outgoing, incoming).wait_send())
    others(lambda e: arrival(e, back_send, back_recv, scanned, returned).wait_send())
    for j in range(1, slow_size):
        first(j).wait_send()
    for j in range(slow_size):
        second(j).wait_send()
        for m in range(2):
            third(j, m).wait_send()
            if crossed and (j, m) != (0, 0):
                cross(j, m).wait_send()

    @pl.when(me < size - 1)
    def _():
        for i in range(tiles):
            halo(i).wait_send()


def shards(queries, key_rows, value_rows, short_taps, decay_rate, residues, skip_gain):
    block, channels = queries.shape
    few, taps = short_taps.shape
    modes = decay_rate.shape[1]
    groups, devs = lax.axis_size("grp"), lax.axis_size("dev")
    size = groups * devs
    part = modes // groups
    table = jnp.asarray(tables(block))
    tiles = channels // min(TILE, channels)
    operands = [key_rows, value_rows, short_taps, decay_rate.T, residues.T, skip_gain.reshape(1, few), table]

    vmem = pl.BlockSpec(memory_space=pltpu.VMEM)
    message = pltpu.VMEM((size, part, few), f32)
    dma = pltpu.SemaphoreType.DMA
    carried = pl.pallas_call(
        whole_kernel,
        in_specs=[pl.BlockSpec(memory_space=pl.ANY)] * len(operands),
        out_specs=vmem,
        out_shape=jax.ShapeDtypeStruct((block, channels), bf16),
        scratch_shapes=[pltpu.VMEM(x.shape, x.dtype) for x in operands]
        + [
            pltpu.VMEM(table.shape, bf16),
            pltpu.VMEM((block, channels), bf16),
            pltpu.VMEM((block, channels), bf16),
            pltpu.VMEM((devs, taps + 4 * modes, few), bf16),
            pltpu.VMEM((block, channels), bf16),
            pltpu.VMEM((2 * block, channels), f32),
            pltpu.VMEM((2 * block, channels), f32),
            pltpu.VMEM((block, channels), f32),
            message, message, message, message,
            dma((len(operands),)), dma((tiles,)), dma((tiles,)), dma((devs // 4 * 6,)), dma((devs // 4 * 6,)),
            dma((size,)), dma((size,)), dma((size,)), dma((size,)),
        ],
        compiler_params=pltpu.CompilerParams(
            collective_id=0, has_side_effects=True, vmem_limit_bytes=56 * 1024 * 1024
        ),
        name="whole",
    )(*operands)
    return (queries.astype(f32) * carried.astype(f32)).astype(bf16)


def solution(mesh):
    return jax.shard_map(
        shards,
        mesh=mesh,
        in_specs=(
            P(("grp", "dev"), None),
            P(("grp", "dev"), None),
            P(("grp", "dev"), None),
            P("dev", None),
            P("dev", None),
            P("dev", None),
            P("dev"),
        ),
        out_specs=P(("grp", "dev"), None),
        check_vma=False,
    )
```

```python
import math

import jax
import jax.numpy as jnp
import ml_dtypes
import numpy as np
from jax import lax
from jax.experimental import pallas as pl
from jax.experimental.pallas import tpu as pltpu
from jax.sharding import PartitionSpec as P

SUB = 8
TILE = 256
f32 = jnp.float32
bf16 = jnp.bfloat16


def tables(block):
    size = 2 * block
    freq = 2 * np.arange(block)[:, None] + 1
    angle = math.pi / size * (freq * np.arange(size)[None, :] % (2 * size))
    forward = np.concatenate([np.cos(angle), -np.sin(angle)], axis=0)
    high = forward.astype(ml_dtypes.bfloat16)
    low = (forward - high.astype(np.float64)).astype(ml_dtypes.bfloat16)
    halves = np.concatenate([high[:, :block], low[:, :block]], axis=1)
    return np.stack([high, halves, (forward.T / block).astype(ml_dtypes.bfloat16)]).astype(np.float32)


def dot(a, b):
    return jnp.dot(a, b, preferred_element_type=f32)


def twice_dot(halves, x):
    return dot(halves, jnp.concatenate([x, x], axis=0))


def turned(x):
    size = x.shape[1]
    eye = lax.broadcasted_iota(jnp.int32, (size, size), 0) == lax.broadcasted_iota(jnp.int32, (size, size), 1)
    eye = jnp.where(eye, 1.0, 0.0).astype(bf16)
    return lax.dot_general(eye, x, (((1,), (1,)), ((), ())), preferred_element_type=f32)


def times(x, h):
    half = x.shape[0] // 2
    xr, xi, hr, hi = x[:half], x[half:], h[:half], h[half:]
    return jnp.concatenate([xr * hr - xi * hi, xr * hi + xi * hr], axis=0)


def lanes_of(pieces):
    return jnp.concatenate(pieces, axis=-1)


def modal_rows(rate, start, block, modes, first):
    step = jnp.exp(-SUB * rate)
    rows = (lax.broadcasted_iota(jnp.int32, (SUB, rate.shape[1]), 0) + first).astype(f32)
    totals = [None] * (block // SUB)
    for m in range(modes):
        term = start[m : m + 1] * jnp.exp(-rate[m : m + 1] * rows)
        factor = jnp.broadcast_to(step[m : m + 1], term.shape)
        for i in range(block // SUB):
            totals[i] = term if m == 0 else totals[i] + term
            term = term * factor
    return jnp.concatenate(totals, axis=0)


def spread(part, index):
    return {"grp": index // part, "dev": index % part}


def whole_kernel(
    key_hbm, value_hbm, taps_hbm, rate_hbm, residue_hbm, gain_hbm, table_hbm, carried_ref,
    key_ref, value_ref, taps_ref, rate_ref, residue_ref, gain_ref, table_ref,
    table, own, prev, params, filtered, tap_spec, local, outgoing, incoming, scanned, returned,
    load_sem, halo_send, halo_recv, gather_send, gather_recv, out_send, out_recv, back_send, back_recv,
):
    block, channels = own.shape
    few, taps = taps_ref.shape
    modes = rate_ref.shape[0]
    groups, devs = lax.axis_size("grp"), lax.axis_size("dev")
    size = groups * devs
    group, dev = lax.axis_index("grp"), lax.axis_index("dev")
    me = group * devs + dev
    part = modes // groups
    width = min(TILE, channels)
    tiles = channels // width
    shards_per_tile = width // few

    def remote(src, dst, send, recv, target):
        return pltpu.make_async_remote_copy(
            src_ref=src, dst_ref=dst, send_sem=send, recv_sem=recv,
            device_id=target, device_id_type=pl.DeviceIdType.MESH,
        )

    def lanes(i, span):
        return pl.ds(pl.multiple_of(i * span, span), span)

    loads = [
        pltpu.make_async_copy(src, dst, load_sem.at[i])
        for i, (src, dst) in enumerate(
            [
                (taps_hbm, taps_ref), (rate_hbm, rate_ref), (residue_hbm, residue_ref), (gain_hbm, gain_ref),
                (key_hbm, key_ref), (value_hbm, value_ref), (table_hbm, table_ref),
            ]
        )
    ]
    for load in loads:
        load.start()

    barrier = pltpu.get_barrier_semaphore()

    def greet(i, carry):
        pl.semaphore_signal(
            barrier, inc=1, device_id=spread(devs, lax.rem(me + i, size)), device_id_type=pl.DeviceIdType.MESH
        )
        return carry

    lax.fori_loop(1, size, greet, 0)

    for load in loads[:4]:
        load.wait()
    rate = rate_ref[...]
    rate_high = rate.astype(bf16)
    rate_low = (rate - rate_high.astype(f32)).astype(bf16).astype(f32)
    rate_high = rate_high.astype(f32)
    weight = residue_ref[...] * jnp.sqrt(2.0 * rate)
    gain = gain_ref[...]
    gain_high = gain.astype(bf16).astype(f32)
    row = lax.broadcasted_iota(jnp.int32, (modes, few), 0)
    gain = jnp.where(row == 0, gain_high, jnp.where(row == 1, gain - gain_high, 0.0))
    params[dev, :taps] = turned(taps_ref[...]).astype(bf16)
    for i, rows in enumerate([rate_high, rate_low, weight, gain]):
        params[dev, taps + i * modes : taps + (i + 1) * modes] = rows.astype(bf16)
    rate = rate_high + rate_low
    own_rate = rate[:part]
    for g in range(1, groups):
        own_rate = jnp.where(group == g, rate[g * part : (g + 1) * part], own_rate)
    decay = jnp.exp(-block * own_rate)
    for load in loads[4:]:
        load.wait()
    table[...] = table_ref[...].astype(bf16)
    for i in range(tiles):
        cols = slice(i * width, (i + 1) * width)
        own[:, cols] = (key_ref[:, cols].astype(f32) * value_ref[:, cols].astype(f32)).astype(bf16)
    pl.semaphore_wait(barrier, size - 1)

    slow_size = devs // 4
    slow, mid, fast = dev // 4, dev // 2 % 2, dev % 2
    crossed = groups == 2
    rows_each = params.shape[1] // 2 if crossed else params.shape[1]

    def slot(s, m, f):
        return s * 4 + m * 2 + f

    def piece(index, whole):
        if whole or not crossed:
            return params.at[index]
        return params.at[index, pl.ds(pl.multiple_of(group * rows_each, 16), rows_each)]

    def gather_copy(index, sem, target_group, target_dev, whole=False):
        return remote(
            piece(index, whole), piece(index, whole), gather_send.at[sem], gather_recv.at[sem],
            {"grp": target_group, "dev": target_dev},
        )

    def source(j, m):
        return slot(lax.rem(slow - j + slow_size, slow_size), mid if m == 0 else 1 - mid, fast)

    def first(j):
        return gather_copy(dev, j, group, slot(lax.rem(slow + j, slow_size), mid, fast))

    def second(j):
        return gather_copy(source(j, 0), slow_size + j, group, slot(slow, 1 - mid, fast))

    def cross(j, m):
        return gather_copy(source(j, m), (2 + m) * slow_size + j, 1 - group, dev)

    def third(j, m):
        return gather_copy(source(j, m), (4 + m) * slow_size + j, group, slot(slow, mid, 1 - fast), True)

    for j in range(1, slow_size):
        first(j).start()
    second(0).start()
    third(0, 0).start()

    next_id = spread(devs, lax.rem(me + 1, size))

    def halo(i):
        return remote(
            own.at[:, lanes(i, width)], prev.at[:, lanes(i, width)], halo_send.at[i], halo_recv.at[i], next_id
        )

    for j in range(1, slow_size):
        first(j).wait_recv()
        second(j).start()
        if crossed:
            cross(j, 0).start()

    @pl.when(me < size - 1)
    def _():
        for i in range(tiles):
            halo(i).start()

    @pl.when(me == 0)
    def _():
        prev[...] = jnp.zeros_like(prev)

    for j in range(1, slow_size):
        if crossed:
            cross(j, 0).wait_recv()
        third(j, 0).start()
    for j in range(slow_size):
        second(j).wait_recv()
        if crossed:
            cross(j, 1).start()
    for j in range(slow_size):
        if crossed:
            cross(j, 1).wait_recv()
        third(j, 1).start()
    for j in range(slow_size):
        third(j, 0).wait_recv()
    for j in range(slow_size):
        third(j, 1).wait_recv()

    def tap_rows(i):
        return lanes_of([params[i * shards_per_tile + n, :taps, :] for n in range(shards_per_tile)])

    def mode_rows(i):
        rows = lanes_of([params[i * shards_per_tile + n, taps:, :].astype(f32) for n in range(shards_per_tile)])
        rate = rows[:modes] + rows[modes : 2 * modes]
        weight = rows[2 * modes : 3 * modes]
        gain = rows[3 * modes : 3 * modes + 1] + rows[3 * modes + 1 : 3 * modes + 2]
        return rate, weight, gain

    def out_copy(target):
        return remote(
            outgoing.at[target], incoming.at[me], out_send.at[target], out_recv.at[me], spread(devs, target)
        )

    def paired(start, stop, step):
        def pair(k, carry):
            return lax.fori_loop(0, 2, lambda n, c: step(start + 2 * k + n, c), carry, unroll=True)

        lax.fori_loop(0, (stop - start) // 2, pair, 0)

    def tap_step(i, carry):
        tap_spec[:, lanes(i, width)] = twice_dot(table[1], tap_rows(i))
        return carry

    paired(0, tiles, tap_step)

    def short_step(i, carry):
        cols = lanes(i, width)

        @pl.when(me > 0)
        def _():
            halo(i).wait_recv()

        x = jnp.concatenate([prev[:, cols], own[:, cols]], axis=0)
        spec = dot(table[0], x)
        rows = dot(table[2, block:], times(spec, tap_spec[:, cols]).astype(bf16)).astype(bf16)
        filtered[:, cols] = rows
        rows = rows.astype(f32)
        rate, _, _ = mode_rows(i)
        step = jnp.exp(-SUB * rate)
        back = (SUB - 1 - lax.broadcasted_iota(jnp.int32, (SUB, width), 0)).astype(f32)
        sums = []
        for m in range(modes):
            factor = jnp.broadcast_to(step[m : m + 1], back.shape)
            total = rows[:SUB]
            for b in range(1, block // SUB):
                total = total * factor + rows[SUB * b : SUB * b + SUB]
            total = total * jnp.exp(-rate[m : m + 1] * back)
            sums.append(jnp.sum(total, axis=0, keepdims=True))
        state = jnp.concatenate(sums, axis=0)
        for n in range(shards_per_tile):
            for g in range(groups):
                target = g * devs + i * shards_per_tile + n
                outgoing[target] = state[g * part : (g + 1) * part, few * n : few * (n + 1)]

                @pl.when(target != me)
                def _():
                    out_copy(target).start()

        return carry

    lax.fori_loop(0, tiles, short_step, 0)

    def local_step(i, carry):
        cols = lanes(i, width)
        rate, weight, gain = mode_rows(i)
        kernel = modal_rows(rate, weight, block, modes, 0)
        kernel_spec = twice_dot(table[1], kernel.astype(bf16))
        rows = filtered[:, cols]
        spec = twice_dot(table[1], rows)
        conv = dot(table[2, :block], times(spec, kernel_spec).astype(bf16))
        local[:, cols] = conv + gain * rows.astype(f32)
        return carry

    paired(0, tiles // 2, local_step)

    incoming[me] = outgoing[me]

    def back_copy(target):
        return remote(
            scanned.at[target], returned.at[me], back_send.at[target], back_recv.at[me], spread(devs, target)
        )

    def arrival(e, send, recv, src, dst):
        return remote(src.at[e], dst.at[e], send.at[e], recv.at[e], spread(devs, e))

    def scan_step(e, carry):
        @pl.when(e != me)
        def _():
            arrival(e, out_send, out_recv, outgoing, incoming).wait_recv()

        scanned[e] = carry

        @pl.when(e != me)
        def _():
            back_copy(e).start()

        return carry * decay + incoming[e]

    lax.fori_loop(0, size, scan_step, jnp.zeros_like(decay))
    returned[me] = scanned[me]

    paired(tiles // 2, tiles, local_step)

    def collect(e, carry):
        @pl.when(e != me)
        def _():
            arrival(e, back_send, back_recv, scanned, returned).wait_recv()

        return carry

    lax.fori_loop(0, size, collect, 0)

    def final_step(i, carry):
        cols = lanes(i, width)
        rate, weight, _ = mode_rows(i)
        state = lanes_of(
            [
                jnp.concatenate([returned[g * devs + i * shards_per_tile + n] for g in range(groups)], axis=0)
                for n in range(shards_per_tile)
            ]
        )
        total = local[:, cols] + modal_rows(rate, weight * state, block, modes, 1)
        carried_ref[:, cols] = total.astype(bf16)
        return carry

    paired(0, tiles, final_step)

    def sent(e, carry):
        @pl.when(e != me)
        def _():
            arrival(e, out_send, out_recv, outgoing, incoming).wait_send()
            arrival(e, back_send, back_recv, scanned, returned).wait_send()

        return carry

    lax.fori_loop(0, size, sent, 0)
    for j in range(1, slow_size):
        first(j).wait_send()
    for j in range(slow_size):
        second(j).wait_send()
        for m in range(2):
            third(j, m).wait_send()
            if crossed and (j, m) != (0, 0):
                cross(j, m).wait_send()

    @pl.when(me < size - 1)
    def _():
        for i in range(tiles):
            halo(i).wait_send()


def shards(queries, key_rows, value_rows, short_taps, decay_rate, residues, skip_gain):
    block, channels = queries.shape
    few, taps = short_taps.shape
    modes = decay_rate.shape[1]
    groups, devs = lax.axis_size("grp"), lax.axis_size("dev")
    size = groups * devs
    part = modes // groups
    table = jnp.asarray(tables(block))
    tiles = channels // min(TILE, channels)
    operands = [key_rows, value_rows, short_taps, decay_rate.T, residues.T, skip_gain.reshape(1, few), table]

    vmem = pl.BlockSpec(memory_space=pltpu.VMEM)
    message = pltpu.VMEM((size, part, few), f32)
    dma = pltpu.SemaphoreType.DMA
    carried = pl.pallas_call(
        whole_kernel,
        in_specs=[pl.BlockSpec(memory_space=pl.ANY)] * len(operands),
        out_specs=vmem,
        out_shape=jax.ShapeDtypeStruct((block, channels), bf16),
        scratch_shapes=[pltpu.VMEM(x.shape, x.dtype) for x in operands]
        + [
            pltpu.VMEM(table.shape, bf16),
            pltpu.VMEM((block, channels), bf16),
            pltpu.VMEM((block, channels), bf16),
            pltpu.VMEM((devs, taps + 4 * modes, few), bf16),
            pltpu.VMEM((block, channels), bf16),
            pltpu.VMEM((2 * block, channels), f32),
            pltpu.VMEM((block, channels), f32),
            message, message, message, message,
            dma((len(operands),)), dma((tiles,)), dma((tiles,)), dma((devs // 4 * 6,)), dma((devs // 4 * 6,)),
            dma((size,)), dma((size,)), dma((size,)), dma((size,)),
        ],
        compiler_params=pltpu.CompilerParams(
            collective_id=0, has_side_effects=True, vmem_limit_bytes=56 * 1024 * 1024
        ),
        name="whole",
    )(*operands)
    return (queries.astype(f32) * carried.astype(f32)).astype(bf16)


def solution(mesh):
    return jax.shard_map(
        shards,
        mesh=mesh,
        in_specs=(
            P(("grp", "dev"), None),
            P(("grp", "dev"), None),
            P(("grp", "dev"), None),
            P("dev", None),
            P("dev", None),
            P("dev", None),
            P("dev"),
        ),
        out_specs=P(("grp", "dev"), None),
        check_vma=False,
    )
```
